32 devices in a mesh: pb: 8 (over z, y), row: 4 (over x, core).
Axes of the slice: x: 2, y: 2, z: 4, core: 2. Of those that a mesh axis runs over, the one named last changes fastest.
Arguments:
- orbitals: bfloat16 [8, 1280, 128], P('pb', 'row'), may hold values from -4 to 4
- interaction: bfloat16 [2, 8, 1280, 1280], P(None, 'pb', 'row'), may hold values from -0.078125 to 0.078125
- pair_list: int32 [8, 3, 2], P('pb'), may hold values from 0 to 7, as said below
- flag_list: int32 [8, 3], P('pb'), may hold values from 0 to 1
- pair_counts: int32 [8], P('pb'), may hold values from 1 to 3, as said below
Outputs:
- exchange_terms: float32 [8, 3, 1280, 128], P('pb', None, 'row')
The draws below stay inside these ranges and needn't reach their ends.
Inputs may be any that keep to these rules, and one draw needn't show every extreme that they name: pair_list[q, s, 1] = (pair_list[q, s, 0] - q) mod 8. `pair_counts`: some q has all 3 slots live.
All inputs are finite; a program needn't handle non-finite values.
Results may differ from the reference program's by a relative error of at most 0.0029.
Values may be sent and summed in bfloat16 or wider, within the bound.
No kernel may reach another device: no remote copies, remote signals or barrier semaphores. Data moves between devices by JAX's collectives and lax.ppermute only.
A program may use at most 64 MiB of HBM per device.

```python
import jax
import jax.numpy as jnp
from jax import lax

NMU = 1280
NB = 64
PAIRS = 3
NQ = 8
NK = 8


def draw_pair_list(key, part):
    first_ids = jax.random.randint(key, (NQ, PAIRS), 0, NK)
    group_index = jnp.arange(NQ, dtype=jnp.int32)[:, None]
    second_ids = (first_ids - group_index) % NK
    return jnp.stack([first_ids, second_ids], axis=2).astype(jnp.int32)


def draw_pair_counts(key, part):
    values = jax.random.randint(key, (NQ,), 1, PAIRS + 1)
    return values.at[0].set(PAIRS).astype(jnp.int32)


def plant(result, own_key, least, high):
    shape = result.shape
    index_at = [jax.random.randint(jax.random.fold_in(own_key, axis), (), 0, shape[axis]) for axis in range(len(shape))]
    result = result.at[tuple(index_at)].set(least)
    longest = shape.index(max(shape))
    index_at[longest] = (index_at[longest] + 1) % shape[longest]
    return result.at[tuple(index_at)].set(high)


def block_scale(stream_key, extent, pieces, low, high):
    gain = 1.0
    for position, blocks in pieces:
        heights = jax.random.uniform(jax.random.fold_in(jax.random.fold_in(stream_key, 6), position), (blocks,), jnp.float32, low / len(pieces), high / len(pieces))
        gain = gain * jnp.repeat(jnp.exp(heights), extent[position] // blocks).reshape((-1,) + (1,) * (len(extent) - 1 - position))
    return gain


def scatter_about(stream_key, dims, scale, reach, pieces=(), kind=jnp.bfloat16):
    entries = jax.random.normal(stream_key, dims, jnp.float32) * scale
    if len(pieces) > 0:
        entries = block_scale(stream_key, dims, pieces, -0.22, 0.18) * entries
    return jnp.clip(entries, min=-reach, max=reach).astype(kind)


def setup_inputs(seed: int = 0) -> dict:
    splits = jax.random.split(jax.random.key(seed), 6)
    orbitals = scatter_about(splits[0], (NK, NMU, 2 * NB), 0.5, 4.0, ((0, 8), (1, 4)))
    interaction = scatter_about(splits[1], (2, NQ, NMU, NMU), (4 * NMU) ** -0.5, 0.078125, ((1, 8), (2, 4)))
    pair_list = draw_pair_list(jax.random.fold_in(splits[5], 71), 0)
    flag_list = plant(jax.random.randint(splits[3], (NQ, PAIRS), 0, 2), jax.random.fold_in(splits[3], 1), 0, 1).astype(jnp.int32)
    pair_counts = draw_pair_counts(jax.random.fold_in(splits[5], 71), 0)
    return {"orbitals": orbitals, "interaction": interaction, "pair_list": pair_list, "flag_list": flag_list, "pair_counts": pair_counts}


def rotate_parts(block):
    half_width = block.shape[1] // 2
    return jnp.concatenate([block[:, half_width:], -block[:, :half_width]], axis=1)


def apply_kernel(kern_real, kern_imag, target):
    half_width = target.shape[1] // 2
    prod_real = jnp.dot(kern_real, target, preferred_element_type=jnp.float32)
    prod_imag = jnp.dot(kern_imag, target, preferred_element_type=jnp.float32)
    return jnp.concatenate([prod_real[:, :half_width] - prod_imag[:, half_width:],
                            prod_real[:, half_width:] + prod_imag[:, :half_width]], axis=1)


def reference(orbitals, interaction, pair_list, flag_list, pair_counts):
    def one_group(inputs):
        w_real, w_imag, group_pairs, group_flags, group_count = inputs
        results = []
        for slot_index in range(PAIRS):
            target = orbitals[group_pairs[slot_index, 0]]
            source = orbitals[group_pairs[slot_index, 1]]
            dens_real = jnp.dot(source, source.T, preferred_element_type=jnp.float32)
            dens_imag = jnp.dot(rotate_parts(source), source.T, preferred_element_type=jnp.float32)
            adjoint = group_flags[slot_index] == 1
            eff_real = jnp.where(adjoint, w_real.T, w_real)
            eff_imag = jnp.where(adjoint, -w_imag.T, w_imag)
            kern_real = (eff_real * dens_real - eff_imag * dens_imag).astype(jnp.bfloat16)
            kern_imag = (eff_real * dens_imag + eff_imag * dens_real).astype(jnp.bfloat16)
            active = (slot_index < group_count).astype(jnp.float32)
            results.append(apply_kernel(kern_real, kern_imag, target) * active)
        return jnp.stack(results)
    return lax.map(one_group, (interaction[0], interaction[1], pair_list, flag_list, pair_counts))
```

```python
import functools

import jax
import jax.numpy as jnp
from jax import lax
from jax.experimental import pallas as pl
from jax.experimental.pallas import tpu as pltpu
from jax.sharding import PartitionSpec as P

CORES = 2


def rotate_parts(block):
    half_width = block.shape[1] // 2
    return jnp.concatenate([block[:, half_width:], -block[:, :half_width]], axis=1)


def apply_kernel(kern_real, kern_imag, target):
    half_width = target.shape[1] // 2
    prod_real = jnp.dot(kern_real, target, preferred_element_type=jnp.float32)
    prod_imag = jnp.dot(kern_imag, target, preferred_element_type=jnp.float32)
    return jnp.concatenate(
        [
            prod_real[:, :half_width] - prod_imag[:, half_width:],
            prod_real[:, half_width:] + prod_imag[:, :half_width],
        ],
        axis=1,
    )


def density(local_rows, all_rows):
    dens_real = jnp.dot(local_rows, all_rows.T, preferred_element_type=jnp.float32)
    dens_imag = jnp.dot(rotate_parts(local_rows), all_rows.T, preferred_element_type=jnp.float32)
    return (dens_real, dens_imag)


def general_shards(orbitals, interaction, pair_list, flag_list, pair_counts):
    slot_total = pair_list.shape[1]
    wanted = jnp.stack([pair_list[0, :, 0], pair_list[0, :, 1]])
    shard_piece = lax.all_gather(orbitals, "pb", axis=0, tiled=True)
    indices = jnp.arange(shard_piece.shape[0], dtype=jnp.int32)
    select = (wanted[:, :, None] == indices[None, None, :]).astype(jnp.bfloat16)
    chosen = jnp.einsum(
        "spi,ird->sprd", select, shard_piece, preferred_element_type=jnp.float32
    ).astype(jnp.bfloat16)
    all_rows = lax.all_gather(chosen, "row", axis=2, tiled=True)
    w_real = interaction[0, 0]
    w_imag = interaction[1, 0]
    active = jnp.arange(slot_total) < pair_counts[0]
    adjoint = flag_list[0] == 1
    turned = lax.all_to_all(interaction[:, 0], "row", split_axis=2, concat_axis=1, tiled=True)
    turned = jnp.swapaxes(turned, 1, 2)
    results = []
    for slot_index in range(slot_total):
        dens_real, dens_imag = density(chosen[1, slot_index], all_rows[1, slot_index])
        eff_real = jnp.where(adjoint[slot_index], turned[0], w_real)
        eff_imag = jnp.where(adjoint[slot_index], -turned[1], w_imag)
        kern_real = (eff_real * dens_real - eff_imag * dens_imag).astype(jnp.bfloat16)
        kern_imag = (eff_real * dens_imag + eff_imag * dens_real).astype(jnp.bfloat16)
        keep_slot = active[slot_index].astype(jnp.float32)
        results.append(apply_kernel(kern_real, kern_imag, all_rows[0, slot_index]) * keep_slot)
    output = jnp.stack(results)
    return output[None]


def ring_position(index, total):
    half = index // 2
    return jnp.where(index % 2 == 0, half, total - 1 - half)


def ring_order(total):
    return list(range(0, total, 2)) + list(range(total - 1, 0, -2))


def rotated(block):
    half = block.shape[1] // 2
    return jnp.concatenate([block[:, half:], -block[:, :half]], axis=1)


def exchange_kernel(steps, total, *refs):
    (place, pairs, flags, counts), refs = refs[:4], refs[4:]
    (w_own, w_core, w_far, w_far_core), refs = refs[:4], refs[4:]
    near, refs = refs[0], refs[1:]
    ring, refs = refs[:steps], refs[steps:]
    swap, refs = refs[:steps], refs[steps:]
    across, across_swap, refs = refs[0], refs[1], refs[2:]
    out, refs = refs[0], refs[1:]
    own_v, core_v, far_v, far_core_v, full, kern, w_sem, orb_sem = refs
    slots, rows, width = out.shape[1:]
    chip = 2 * rows
    wide = rows + 64
    me, x, c = place[0], place[1], place[2]

    w_copies = [
        pltpu.make_async_copy(src, dst, w_sem.at[k])
        for k, (src, dst) in enumerate(
            [(w_own.at[:, 0], own_v), (w_core, core_v), (w_far, far_v), (w_far_core, far_core_v)]
        )
    ]

    def fetch(which, slot):
        momentum = pairs[0, slot, which]
        spot = jnp.where(momentum % 2 == 0, momentum // 2, total - 1 - momentum // 2)
        gap = lax.rem(spot - me + total, total)
        dst = full.at[which, slot]
        sem = orb_sem.at[which, slot]

        def start(src, when):
            @pl.when(when)
            def _():
                pltpu.make_async_copy(src, dst, sem).start()

        start(near, gap == 0)
        for k in range(1, steps + 1):
            start(ring[k - 1], gap == jnp.where(c == 0, total - k, k))
            start(swap[k - 1], gap == jnp.where(c == 0, k, total - k))

        @pl.when(gap == steps + 1)
        def _():
            for piece, core in ((across, c), (across_swap, 1 - c)):
                for part, chip_x in ((0, x), (1, 1 - x)):
                    at = pl.multiple_of((2 * chip_x + core) * rows, rows)
                    pltpu.make_async_copy(
                        piece.at[pl.ds(part * rows, rows)], dst.at[pl.ds(at, rows)], sem
                    ).start()

    def arrive(which, slot):
        pltpu.make_async_copy(near, full.at[which, slot], orb_sem.at[which, slot]).wait()

    fetch(1, 0)
    for copy in w_copies:
        copy.start()
    fetch(0, 0)
    for slot in range(1, slots):
        fetch(1, slot)
        fetch(0, slot)

    def multiply(w_real, w_imag, dens):
        count = w_real.shape[0]
        w_real, w_imag = w_real.astype(jnp.float32), w_imag.astype(jnp.float32)
        dens_real, dens_imag = dens[:count], dens[count:]
        return (
            (w_real * dens_real - w_imag * dens_imag).astype(jnp.bfloat16),
            (w_real * dens_imag + w_imag * dens_real).astype(jnp.bfloat16),
        )

    def direct(slot):
        mine = pl.multiple_of((2 * x + c) * rows, rows)
        local = full[1, slot, pl.ds(mine, rows)]
        left = jnp.concatenate([local, rotated(local)], axis=0)
        step = 256
        points = full.shape[2]
        total_out = jnp.zeros((rows, width), jnp.float32)
        for at in range(0, points, step):
            dens = lax.dot_general(
                left,
                full[1, slot, at : at + step],
                (((1,), (1,)), ((), ())),
                preferred_element_type=jnp.float32,
            )
            kern_real, kern_imag = multiply(
                own_v[0, :, at : at + step], own_v[1, :, at : at + step], dens
            )
            target = full[0, slot, at : at + step]
            total_out += jnp.dot(kern_real, target, preferred_element_type=jnp.float32)
            total_out += jnp.dot(kern_imag, -rotated(target), preferred_element_type=jnp.float32)
        out[0, slot] = total_out

    def adjoint(slot):
        lane = pl.multiple_of(c * (chip - wide), 128)
        start = pl.multiple_of(x * chip + c * (chip - wide), 128)
        right = full[1, slot, pl.ds(start, wide)]
        total_out = jnp.zeros((width, wide), jnp.float32)
        for px, pc, block, offset in (
            (x, c, own_v, start),
            (x, 1 - c, core_v, lane),
            (1 - x, c, far_v, lane),
            (1 - x, 1 - c, far_core_v, lane),
        ):
            at = pl.multiple_of((2 * px + pc) * rows, rows)
            local = full[1, slot, pl.ds(at, rows)]
            left = jnp.concatenate([local, rotated(local)], axis=0)
            dens = lax.dot_general(
                left, right, (((1,), (1,)), ((), ())), preferred_element_type=jnp.float32
            )
            kern_real, kern_imag = multiply(
                block[0, :, pl.ds(offset, wide)], block[1, :, pl.ds(offset, wide)], dens
            )
            target = full[0, slot, pl.ds(at, rows)]
            over_rows = (((0,), (0,)), ((), ()))
            total_out += lax.dot_general(
                target, kern_real, over_rows, preferred_element_type=jnp.float32
            )
            total_out += lax.dot_general(
                rotated(target), kern_imag, over_rows, preferred_element_type=jnp.float32
            )
        kern[...] = total_out.T
        out[0, slot] = kern[pl.ds(pl.multiple_of(c * (wide - rows), 8), rows)]

    for slot in range(slots):
        arrive(1, slot)
        if slot == 0:
            for copy in w_copies:
                copy.wait()
        arrive(0, slot)
        live = slot < counts[0]

        @pl.when(jnp.logical_and(live, flags[0, slot] != 1))
        def _(slot=slot):
            direct(slot)

        @pl.when(jnp.logical_and(live, flags[0, slot] == 1))
        def _(slot=slot):
            adjoint(slot)

        @pl.when(jnp.logical_not(live))
        def _(slot=slot):
            out[0, slot] = jnp.zeros((rows, width), jnp.float32)


def paired_shards(total, orbitals, interaction, pair_list, flag_list, pair_counts):
    _, rows, width = orbitals.shape
    slots = pair_list.shape[1]
    points = interaction.shape[3]
    chip = CORES * rows
    row = lax.axis_index("row")
    x, c = row // CORES, row % CORES
    me = ring_position(lax.axis_index("pb"), total)
    order = ring_order(total)
    row_total = 2 * CORES

    def other_core(value):
        return lax.ppermute(value, "row", [(r, r ^ 1) for r in range(row_total)])

    def other_chip(value):
        return lax.ppermute(value, "row", [(r, r ^ CORES) for r in range(row_total)])

    def along_ring(value):
        moves = []
        for place in range(total):
            for r in range(row_total):
                step = 1 if r % CORES == 0 else -1
                target = order[(place + step) % total]
                moves.append((order[place] * row_total + r, target * row_total + r))
        return lax.ppermute(value, ("pb", "row"), moves)

    def across_ring(value):
        half = total // 2
        moves = [
            (order[p] * row_total + r, order[(p + half) % total] * row_total + r)
            for p in range(total)
            for r in range(row_total)
        ]
        return lax.ppermute(value, ("pb", "row"), moves)

    def after(value, *earlier):
        return lax.optimization_barrier((value, *earlier))[0]

    own = orbitals[0]
    w_block = interaction[:, 0]
    near_other = other_core(own)
    far = other_chip(own)
    w_away = lax.dynamic_slice_in_dim(w_block, (1 - x) * chip, chip, axis=2)
    w_far = other_chip(after(w_away, near_other))
    far_other = other_core(far)
    turns = [[0, 1, 2, 3], [1, 0, 3, 2], [2, 3, 0, 1], [3, 2, 1, 0]]
    parts = [own, near_other, far, far_other]
    near = jnp.concatenate(parts)
    for case in range(1, 4):
        near = jnp.where(row == case, jnp.concatenate([parts[t] for t in turns[case]]), near)
    steps = total // 2 - 1
    ring = [along_ring(near)]
    across = across_ring(jnp.concatenate([own, far]))
    for k in range(1, steps):
        ring.append(along_ring(after(ring[-1], across) if k == steps - 1 else ring[-1]))
    swap = [other_core(after(ring[k], *ring[k + 1 : k + 2])) for k in range(steps)]
    across_swap = other_core(across)
    w_mine = lax.dynamic_slice_in_dim(after(w_block, ring[0]), x * chip, chip, axis=2)
    w_core = other_core(w_mine)
    w_far_core = other_core(after(w_far, ring[-1]))

    place = jnp.stack([me, x, c]).astype(jnp.int32)
    anywhere = pl.BlockSpec(memory_space=pltpu.HBM)
    scalars = pl.BlockSpec(memory_space=pltpu.SMEM)
    orbital_pieces = [
        pltpu.with_memory_space_constraint(piece, pltpu.HBM)
        for piece in (near, *ring, *swap, across, across_swap)
    ]
    wide = rows + 64
    return pl.pallas_call(
        functools.partial(exchange_kernel, steps, total),
        out_shape=jax.ShapeDtypeStruct((1, slots, rows, width), jnp.float32),
        in_specs=[scalars] * 4 + [anywhere] * (4 + len(orbital_pieces)),
        out_specs=pl.BlockSpec(memory_space=pltpu.VMEM),
        scratch_shapes=[
            pltpu.VMEM((2, rows, points), jnp.bfloat16),
            pltpu.VMEM((2, rows, chip), jnp.bfloat16),
            pltpu.VMEM((2, rows, chip), jnp.bfloat16),
            pltpu.VMEM((2, rows, chip), jnp.bfloat16),
            pltpu.VMEM((2, slots, points, width), jnp.bfloat16),
            pltpu.VMEM((wide, width), jnp.float32),
            pltpu.SemaphoreType.DMA((4,)),
            pltpu.SemaphoreType.DMA((2, slots)),
        ],
        compiler_params=pltpu.CompilerParams(vmem_limit_bytes=16 * 2**20),
        cost_estimate=pl.CostEstimate(
            flops=slots * rows * points * width * 8, bytes_accessed=8 * 2**20, transcendentals=0
        ),
    )(
        place, pair_list, flag_list, pair_counts,
        interaction, w_core, w_far, w_far_core, *orbital_pieces,
    )


def solution(mesh):
    total, row_total = mesh.shape["pb"], mesh.shape["row"]

    def shards(orbitals, interaction, pair_list, flag_list, pair_counts):
        rows, width = orbitals.shape[1:]
        fits = total * interaction.shape[3] * width * 2 <= 8 * 2**20
        aligned = rows % 64 == 0 and (CORES * rows) % 128 == 0 and (rows + 64) % 128 == 0
        if row_total == 2 * CORES and total % 2 == 0 and total >= 4 and fits and aligned:
            return paired_shards(
                total, orbitals, interaction, pair_list, flag_list, pair_counts
            )
        return general_shards(orbitals, interaction, pair_list, flag_list, pair_counts)

    return jax.shard_map(
        shards,
        mesh=mesh,
        in_specs=(
            P("pb", "row", None),
            P(None, "pb", "row", None),
            P("pb", None, None),
            P("pb", None),
            P("pb"),
        ),
        out_specs=P("pb", None, "row", None),
        check_vma=False,
    )
```

```python
import functools

import jax
import jax.numpy as jnp
from jax import lax
from jax.experimental import pallas as pl
from jax.experimental.pallas import tpu as pltpu
from jax.sharding import PartitionSpec as P

CORES = 2


def rotate_parts(block):
    half_width = block.shape[1] // 2
    return jnp.concatenate([block[:, half_width:], -block[:, :half_width]], axis=1)


def apply_kernel(kern_real, kern_imag, target):
    half_width = target.shape[1] // 2
    prod_real = jnp.dot(kern_real, target, preferred_element_type=jnp.float32)
    prod_imag = jnp.dot(kern_imag, target, preferred_element_type=jnp.float32)
    return jnp.concatenate(
        [
            prod_real[:, :half_width] - prod_imag[:, half_width:],
            prod_real[:, half_width:] + prod_imag[:, :half_width],
        ],
        axis=1,
    )


def density(local_rows, all_rows):
    dens_real = jnp.dot(local_rows, all_rows.T, preferred_element_type=jnp.float32)
    dens_imag = jnp.dot(rotate_parts(local_rows), all_rows.T, preferred_element_type=jnp.float32)
    return (dens_real, dens_imag)


def general_shards(orbitals, interaction, pair_list, flag_list, pair_counts):
    slot_total = pair_list.shape[1]
    wanted = jnp.stack([pair_list[0, :, 0], pair_list[0, :, 1]])
    shard_piece = lax.all_gather(orbitals, "pb", axis=0, tiled=True)
    indices = jnp.arange(shard_piece.shape[0], dtype=jnp.int32)
    select = (wanted[:, :, None] == indices[None, None, :]).astype(jnp.bfloat16)
    chosen = jnp.einsum(
        "spi,ird->sprd", select, shard_piece, preferred_element_type=jnp.float32
    ).astype(jnp.bfloat16)
    all_rows = lax.all_gather(chosen, "row", axis=2, tiled=True)
    w_real = interaction[0, 0]
    w_imag = interaction[1, 0]
    active = jnp.arange(slot_total) < pair_counts[0]
    adjoint = flag_list[0] == 1
    turned = lax.all_to_all(interaction[:, 0], "row", split_axis=2, concat_axis=1, tiled=True)
    turned = jnp.swapaxes(turned, 1, 2)
    results = []
    for slot_index in range(slot_total):
        dens_real, dens_imag = density(chosen[1, slot_index], all_rows[1, slot_index])
        eff_real = jnp.where(adjoint[slot_index], turned[0], w_real)
        eff_imag = jnp.where(adjoint[slot_index], -turned[1], w_imag)
        kern_real = (eff_real * dens_real - eff_imag * dens_imag).astype(jnp.bfloat16)
        kern_imag = (eff_real * dens_imag + eff_imag * dens_real).astype(jnp.bfloat16)
        keep_slot = active[slot_index].astype(jnp.float32)
        results.append(apply_kernel(kern_real, kern_imag, all_rows[0, slot_index]) * keep_slot)
    output = jnp.stack(results)
    return output[None]


def ring_position(index, total):
    half = index // 2
    return jnp.where(index % 2 == 0, half, total - 1 - half)


def ring_order(total):
    return list(range(0, total, 2)) + list(range(total - 1, 0, -2))


def rotated(block):
    half = block.shape[1] // 2
    return jnp.concatenate([block[:, half:], -block[:, :half]], axis=1)


def exchange_kernel(steps, total, *refs):
    (place, pairs, flags, counts), refs = refs[:4], refs[4:]
    (w_own, w_core, w_far, w_far_core), refs = refs[:4], refs[4:]
    near, refs = refs[:2], refs[2:]
    ring, refs = refs[: 2 * steps], refs[2 * steps :]
    swap, refs = refs[: 2 * steps], refs[2 * steps :]
    last, refs = refs[:2], refs[2:]
    out, eff, full, w_sem, orb_sem = refs
    slots, rows, width = out.shape[1:]
    points = full.shape[2]
    chip = 2 * rows
    wide = rows + 64
    me, x, c = place[0], place[1], place[2]

    def fetch(slot):
        turned = flags[0, slot] == 1
        for which in (1, 0):
            momentum = pairs[0, slot, which]
            spot = jnp.where(momentum % 2 == 0, momentum // 2, total - 1 - momentum // 2)
            gap = lax.rem(spot - me + total, total)
            dst, sem = full.at[which, slot], orb_sem.at[which, slot]

            def bring(waves, dst=dst, sem=sem):
                for wave in range(2):
                    at = jnp.where(turned, wave, jnp.where(wave == 0, x, 1 - x)) * chip
                    pltpu.make_async_copy(
                        waves[wave], dst.at[pl.ds(pl.multiple_of(at, chip), chip)], sem
                    ).start()

            pl.when(gap == 0)(functools.partial(bring, near))
            for k in range(1, steps + 1):
                own = gap == jnp.where(c == 0, total - k, k)
                other = gap == jnp.where(c == 0, k, total - k)
                pl.when(own)(functools.partial(bring, ring[2 * k - 2 : 2 * k]))
                pl.when(other)(functools.partial(bring, swap[2 * k - 2 : 2 * k]))
            pl.when(gap == steps + 1)(functools.partial(bring, last))

    def arrive(which, slot):
        pltpu.make_async_copy(
            full.at[which, slot], full.at[which, slot], orb_sem.at[which, slot]
        ).wait()

    fetch(0)
    eff_copy = pltpu.make_async_copy(w_own.at[:, 0], eff.at[0], w_sem)
    eff_copy.start()
    for slot in range(1, slots):
        fetch(slot)
    any_turned = False
    for slot in range(slots):
        any_turned = jnp.logical_or(
            any_turned, jnp.logical_and(slot < counts[0], flags[0, slot] == 1)
        )
    for core in range(CORES):

        @pl.when(jnp.logical_and(any_turned, c == core))
        def _(core=core):
            first = core * (chip - wide)
            start = pl.multiple_of(x * chip + first, 128)
            skip = core * (wide - rows)
            for block, lanes, at in (
                (w_own.at[:, 0], pl.ds(start, wide), core * rows),
                (w_core, slice(first, first + wide), (1 - core) * rows),
                (w_far, slice(first, first + wide), chip + core * rows),
                (w_far_core, slice(first, first + wide), chip + (1 - core) * rows),
            ):
                eff[1, 0, :, at : at + rows] = block[0, :, lanes].T[skip : skip + rows]
                eff[1, 1, :, at : at + rows] = -block[1, :, lanes].T[skip : skip + rows]

    eff_copy.wait()

    def compute(slot, carry):
        arrive(1, slot)
        arrive(0, slot)
        live = slot < counts[0]

        @pl.when(live)
        def _():
            flag = flags[0, slot]
            mine = pl.multiple_of(jnp.where(flag == 1, c, 2 * x + c) * rows, rows)
            local = full[1, slot, pl.ds(mine, rows)]
            left = jnp.concatenate([local, rotated(local)], axis=0)
            step = 128
            result = jnp.zeros((rows, width), jnp.float32)
            for at in range(0, points, step):
                dens = lax.dot_general(
                    left,
                    full[1, slot, at : at + step],
                    (((1,), (1,)), ((), ())),
                    preferred_element_type=jnp.float32,
                )
                dens_real, dens_imag = dens[:rows], dens[rows:]
                eff_real = eff[flag, 0, :, at : at + step].astype(jnp.float32)
                eff_imag = eff[flag, 1, :, at : at + step].astype(jnp.float32)
                kern_real = (eff_real * dens_real - eff_imag * dens_imag).astype(jnp.bfloat16)
                kern_imag = (eff_real * dens_imag + eff_imag * dens_real).astype(jnp.bfloat16)
                target = full[0, slot, at : at + step]
                result += jnp.dot(kern_real, target, preferred_element_type=jnp.float32)
                result += jnp.dot(
                    kern_imag, -rotated(target), preferred_element_type=jnp.float32
                )
            out[0, slot] = result

        @pl.when(jnp.logical_not(live))
        def _():
            out[0, slot] = jnp.zeros((rows, width), jnp.float32)

        return carry

    lax.fori_loop(0, slots, compute, 0)


def paired_shards(total, orbitals, interaction, pair_list, flag_list, pair_counts):
    _, rows, width = orbitals.shape
    slots = pair_list.shape[1]
    points = interaction.shape[3]
    chip = CORES * rows
    row = lax.axis_index("row")
    x, c = row // CORES, row % CORES
    me = ring_position(lax.axis_index("pb"), total)
    order = ring_order(total)
    row_total = 2 * CORES

    def other_core(value):
        return lax.ppermute(value, "row", [(r, r ^ 1) for r in range(row_total)])

    def other_chip(value):
        return lax.ppermute(value, "row", [(r, r ^ CORES) for r in range(row_total)])

    def along_ring(value):
        moves = []
        for place in range(total):
            for r in range(row_total):
                step = 1 if r % CORES == 0 else -1
                target = order[(place + step) % total]
                moves.append((order[place] * row_total + r, target * row_total + r))
        return lax.ppermute(value, ("pb", "row"), moves)

    def in_order(mine, other):
        return jnp.where(
            c == 0, jnp.concatenate([mine, other]), jnp.concatenate([other, mine])
        )

    def after(value, *earlier):
        return lax.optimization_barrier((value, *earlier))[0]

    own = orbitals[0]
    w_block = interaction[:, 0]
    far = other_chip(own)
    near_other = other_core(own)
    w_away = lax.dynamic_slice_in_dim(w_block, (1 - x) * chip, chip, axis=2)
    w_mine = lax.dynamic_slice_in_dim(w_block, x * chip, chip, axis=2)
    w_far = other_chip(after(w_away, far))
    near = [in_order(own, near_other), in_order(far, other_core(after(far, w_away, w_mine)))]
    steps = total // 2 - 1
    first, second = [near[0]], [near[1]]
    for _ in range(steps + 1):
        first.append(along_ring(first[-1]))
        second.append(along_ring(second[-1]))
    ring, swap = [], []
    for k in range(1, steps + 1):
        ring += [first[k], second[k]]
        swap += [other_core(after(first[k], first[steps+1])), other_core(after(second[k], second[steps+1]))]
    last = [first[steps + 1], second[steps + 1]]
    w_core = other_core(after(w_mine, first[steps+1]))
    w_far_core = other_core(after(w_far, second[steps+1]))

    place = jnp.stack([me, x, c]).astype(jnp.int32)
    in_hbm = pl.BlockSpec(memory_space=pltpu.HBM)
    in_vmem = pl.BlockSpec(memory_space=pltpu.VMEM)
    scalars = pl.BlockSpec(memory_space=pltpu.SMEM)
    pieces = [
        pltpu.with_memory_space_constraint(piece, pltpu.HBM)
        for piece in (*near, *ring, *swap, *last)
    ]
    w_pieces = [pltpu.with_memory_space_constraint(piece, pltpu.VMEM) for piece in (interaction, w_core, w_far, w_far_core)]
    return pl.pallas_call(
        functools.partial(exchange_kernel, steps, total),
        out_shape=jax.ShapeDtypeStruct((1, slots, rows, width), jnp.float32),
        in_specs=[scalars] * 4 + [in_vmem] * 4 + [in_hbm] * len(pieces),
        out_specs=in_vmem,
        scratch_shapes=[
            pltpu.VMEM((2, 2, rows, points), jnp.bfloat16),
            pltpu.VMEM((2, slots, points, width), jnp.bfloat16),
            pltpu.SemaphoreType.DMA,
            pltpu.SemaphoreType.DMA((2, slots)),
        ],
        compiler_params=pltpu.CompilerParams(vmem_limit_bytes=24 * 2**20),
        cost_estimate=pl.CostEstimate(
            flops=slots * rows * points * width * 8, bytes_accessed=8 * 2**20, transcendentals=0
        ),
    )(
        place, pair_list, flag_list, pair_counts,
        *w_pieces, *pieces,
    )


def solution(mesh):
    total, row_total = mesh.shape["pb"], mesh.shape["row"]

    def shards(orbitals, interaction, pair_list, flag_list, pair_counts):
        rows, width = orbitals.shape[1:]
        fits = total * interaction.shape[3] * width * 2 <= 8 * 2**20
        aligned = rows % 64 == 0 and (CORES * rows) % 128 == 0 and (rows + 64) % 128 == 0
        if row_total == 2 * CORES and total % 2 == 0 and total >= 4 and fits and aligned:
            return paired_shards(
                total, orbitals, interaction, pair_list, flag_list, pair_counts
            )
        return general_shards(orbitals, interaction, pair_list, flag_list, pair_counts)

    return jax.shard_map(
        shards,
        mesh=mesh,
        in_specs=(
            P("pb", "row", None),
            P(None, "pb", "row", None),
            P("pb", None, None),
            P("pb", None),
            P("pb"),
        ),
        out_specs=P("pb", None, "row", None),
        check_vma=False,
    )
```

```python
import functools

import jax
import jax.numpy as jnp
from jax import lax
from jax.experimental import pallas as pl
from jax.experimental.pallas import tpu as pltpu
from jax.sharding import PartitionSpec as P

CORES = 2


def rotate_parts(block):
    half_width = block.shape[1] // 2
    return jnp.concatenate([block[:, half_width:], -block[:, :half_width]], axis=1)


def apply_kernel(kern_real, kern_imag, target):
    half_width = target.shape[1] // 2
    prod_real = jnp.dot(kern_real, target, preferred_element_type=jnp.float32)
    prod_imag = jnp.dot(kern_imag, target, preferred_element_type=jnp.float32)
    return jnp.concatenate(
        [
            prod_real[:, :half_width] - prod_imag[:, half_width:],
            prod_real[:, half_width:] + prod_imag[:, :half_width],
        ],
        axis=1,
    )


def density(local_rows, all_rows):
    dens_real = jnp.dot(local_rows, all_rows.T, preferred_element_type=jnp.float32)
    dens_imag = jnp.dot(rotate_parts(local_rows), all_rows.T, preferred_element_type=jnp.float32)
    return (dens_real, dens_imag)


def general_shards(orbitals, interaction, pair_list, flag_list, pair_counts):
    slot_total = pair_list.shape[1]
    wanted = jnp.stack([pair_list[0, :, 0], pair_list[0, :, 1]])
    shard_piece = lax.all_gather(orbitals, "pb", axis=0, tiled=True)
    indices = jnp.arange(shard_piece.shape[0], dtype=jnp.int32)
    select = (wanted[:, :, None] == indices[None, None, :]).astype(jnp.bfloat16)
    chosen = jnp.einsum(
        "spi,ird->sprd", select, shard_piece, preferred_element_type=jnp.float32
    ).astype(jnp.bfloat16)
    all_rows = lax.all_gather(chosen, "row", axis=2, tiled=True)
    w_real = interaction[0, 0]
    w_imag = interaction[1, 0]
    active = jnp.arange(slot_total) < pair_counts[0]
    adjoint = flag_list[0] == 1
    turned = lax.all_to_all(interaction[:, 0], "row", split_axis=2, concat_axis=1, tiled=True)
    turned = jnp.swapaxes(turned, 1, 2)
    results = []
    for slot_index in range(slot_total):
        dens_real, dens_imag = density(chosen[1, slot_index], all_rows[1, slot_index])
        eff_real = jnp.where(adjoint[slot_index], turned[0], w_real)
        eff_imag = jnp.where(adjoint[slot_index], -turned[1], w_imag)
        kern_real = (eff_real * dens_real - eff_imag * dens_imag).astype(jnp.bfloat16)
        kern_imag = (eff_real * dens_imag + eff_imag * dens_real).astype(jnp.bfloat16)
        keep_slot = active[slot_index].astype(jnp.float32)
        results.append(apply_kernel(kern_real, kern_imag, all_rows[0, slot_index]) * keep_slot)
    output = jnp.stack(results)
    return output[None]


def ring_position(index, total):
    half = index // 2
    return jnp.where(index % 2 == 0, half, total - 1 - half)


def ring_order(total):
    return list(range(0, total, 2)) + list(range(total - 1, 0, -2))


def rotated(block):
    half = block.shape[1] // 2
    return jnp.concatenate([block[:, half:], -block[:, :half]], axis=1)


def exchange_kernel(steps, total, *refs):
    (pairs, flags, counts), refs = refs[:3], refs[3:]
    (w_own, w_core, w_far, w_far_core), refs = refs[:4], refs[4:]
    near, refs = refs[:2], refs[2:]
    ring, refs = refs[: 2 * steps], refs[2 * steps :]
    swap, refs = refs[: 2 * steps], refs[2 * steps :]
    last, refs = refs[:2], refs[2:]
    out, eff, full, w_sem, orb_sem = refs
    slots, rows, width = out.shape[1:]
    points = full.shape[2]
    chip = 2 * rows
    wide = rows + 64
    row = lax.axis_index("row")
    x, c = row // CORES, row % CORES
    me = ring_position(lax.axis_index("pb"), total)

    def fetch(slot):
        turned = flags[0, slot] == 1
        for which in (1, 0):
            momentum = pairs[0, which, slot]
            spot = jnp.where(momentum % 2 == 0, momentum // 2, total - 1 - momentum // 2)
            gap = lax.rem(spot - me + total, total)
            dst, sem = full.at[which, slot], orb_sem.at[which, slot]

            def bring(waves, dst=dst, sem=sem):
                for wave in range(2):
                    at = jnp.where(turned, wave, jnp.where(wave == 0, x, 1 - x)) * chip
                    pltpu.make_async_copy(
                        waves[wave], dst.at[pl.ds(pl.multiple_of(at, chip), chip)], sem
                    ).start()

            pl.when(gap == 0)(functools.partial(bring, near))
            for k in range(1, steps + 1):
                own = gap == jnp.where(c == 0, total - k, k)
                other = gap == jnp.where(c == 0, k, total - k)
                pl.when(own)(functools.partial(bring, ring[2 * k - 2 : 2 * k]))
                pl.when(other)(functools.partial(bring, swap[2 * k - 2 : 2 * k]))
            pl.when(gap == steps + 1)(functools.partial(bring, last))

    def arrive(which, slot):
        pltpu.make_async_copy(
            full.at[which, slot], full.at[which, slot], orb_sem.at[which, slot]
        ).wait()

    fetch(0)
    eff_copy = pltpu.make_async_copy(w_own.at[:, 0], eff.at[0], w_sem)
    eff_copy.start()
    for slot in range(1, slots):
        fetch(slot)
    any_turned = False
    for slot in range(slots):
        any_turned = jnp.logical_or(
            any_turned, jnp.logical_and(slot < counts[0], flags[0, slot] == 1)
        )
    for core in range(CORES):

        @pl.when(jnp.logical_and(any_turned, c == core))
        def _(core=core):
            first = core * (chip - wide)
            start = pl.multiple_of(x * chip + first, 128)
            skip = core * (wide - rows)
            for block, lanes, at in (
                (w_own.at[:, 0], pl.ds(start, wide), core * rows),
                (w_core, slice(first, first + wide), (1 - core) * rows),
                (w_far, slice(first, first + wide), chip + core * rows),
                (w_far_core, slice(first, first + wide), chip + (1 - core) * rows),
            ):
                eff[1, 0, :, at : at + rows] = block[0, :, lanes].T[skip : skip + rows]
                eff[1, 1, :, at : at + rows] = -block[1, :, lanes].T[skip : skip + rows]

    eff_copy.wait()

    def compute(slot, carry):
        arrive(1, slot)
        arrive(0, slot)
        live = slot < counts[0]

        @pl.when(live)
        def _():
            flag = flags[0, slot]
            mine = pl.multiple_of(jnp.where(flag == 1, c, 2 * x + c) * rows, rows)
            local = full[1, slot, pl.ds(mine, rows)]
            left = jnp.concatenate([local, rotated(local)], axis=0)
            step = 128
            result = jnp.zeros((rows, width), jnp.float32)
            for at in range(0, points, step):
                dens = lax.dot_general(
                    left,
                    full[1, slot, at : at + step],
                    (((1,), (1,)), ((), ())),
                    preferred_element_type=jnp.float32,
                )
                dens_real, dens_imag = dens[:rows], dens[rows:]
                eff_real = eff[flag, 0, :, at : at + step].astype(jnp.float32)
                eff_imag = eff[flag, 1, :, at : at + step].astype(jnp.float32)
                kern_real = (eff_real * dens_real - eff_imag * dens_imag).astype(jnp.bfloat16)
                kern_imag = (eff_real * dens_imag + eff_imag * dens_real).astype(jnp.bfloat16)
                target = full[0, slot, at : at + step]
                result += jnp.dot(kern_real, target, preferred_element_type=jnp.float32)
                result += jnp.dot(
                    kern_imag, -rotated(target), preferred_element_type=jnp.float32
                )
            out[0, slot] = result

        @pl.when(jnp.logical_not(live))
        def _():
            out[0, slot] = jnp.zeros((rows, width), jnp.float32)

        return carry

    lax.fori_loop(0, slots, compute, 0)


def paired_shards(total, orbitals, interaction, pair_list, flag_list, pair_counts):
    _, rows, width = orbitals.shape
    slots = pair_list.shape[1]
    points = interaction.shape[3]
    chip = CORES * rows
    row = lax.axis_index("row")
    x, c = row // CORES, row % CORES
    order = ring_order(total)
    row_total = 2 * CORES

    def other_core(value):
        return lax.ppermute(value, "row", [(r, r ^ 1) for r in range(row_total)])

    def other_chip(value):
        return lax.ppermute(value, "row", [(r, r ^ CORES) for r in range(row_total)])

    def along_ring(value):
        moves = []
        for place in range(total):
            for r in range(row_total):
                step = 1 if r % CORES == 0 else -1
                target = order[(place + step) % total]
                moves.append((order[place] * row_total + r, target * row_total + r))
        return lax.ppermute(value, ("pb", "row"), moves)

    def in_order(mine, other):
        return jnp.where(
            c == 0, jnp.concatenate([mine, other]), jnp.concatenate([other, mine])
        )

    def after(value, *earlier):
        return lax.optimization_barrier((value, *earlier))[0]

    own = orbitals[0]
    w_block = interaction[:, 0]
    far = other_chip(own)
    near_other = other_core(own)
    near = [in_order(own, near_other)]
    w_away = lax.dynamic_slice_in_dim(w_block, (1 - x) * chip, chip, axis=2)
    w_far = other_chip(after(w_away, far))
    near.append(in_order(far, other_core(after(far, w_away))))
    steps = total // 2 - 1
    first, second = [near[0]], [near[1]]
    swap_first, swap_second = [], []
    for k in range(steps + 1):
        if k >= 2:
            swap_first.append(other_core(first[k - 1]))
            swap_second.append(other_core(second[k - 1]))
        first.append(along_ring(after(first[-1], swap_second[0]) if k == 3 else first[-1]))
        second.append(along_ring(after(second[-1], swap_first[0]) if k == 3 else second[-1]))
    ring = [wave[k] for k in range(1, steps + 1) for wave in (first, second)]
    last = [first[steps + 1], second[steps + 1]]
    for k in range(len(swap_first) + 1, steps + 1):
        swap_first.append(other_core(after(first[k], last[0])))
        swap_second.append(other_core(after(second[k], last[1])))
    swap = [wave[k] for k in range(steps) for wave in (swap_first, swap_second)]
    w_far_core = other_core(after(w_far, last[1]))
    w_mine = lax.dynamic_slice_in_dim(w_block, x * chip, chip, axis=2)
    w_core = other_core(after(w_mine, last[0]))

    in_hbm = pl.BlockSpec(memory_space=pltpu.HBM)
    in_vmem = pl.BlockSpec(memory_space=pltpu.VMEM)
    scalars = pl.BlockSpec(memory_space=pltpu.SMEM)
    pieces = [
        pltpu.with_memory_space_constraint(piece, pltpu.HBM)
        for piece in (*near, *ring, *swap, *last)
    ]
    w_pieces = [pltpu.with_memory_space_constraint(piece, pltpu.VMEM) for piece in (interaction, w_core, w_far, w_far_core)]
    return pl.pallas_call(
        functools.partial(exchange_kernel, steps, total),
        out_shape=jax.ShapeDtypeStruct((1, slots, rows, width), jnp.float32),
        in_specs=[scalars] * 3 + [in_vmem] * 4 + [in_hbm] * len(pieces),
        out_specs=in_vmem,
        scratch_shapes=[
            pltpu.VMEM((2, 2, rows, points), jnp.bfloat16),
            pltpu.VMEM((2, slots, points, width), jnp.bfloat16),
            pltpu.SemaphoreType.DMA,
            pltpu.SemaphoreType.DMA((2, slots)),
        ],
        compiler_params=pltpu.CompilerParams(vmem_limit_bytes=24 * 2**20),
        cost_estimate=pl.CostEstimate(
            flops=slots * rows * points * width * 8, bytes_accessed=8 * 2**20, transcendentals=0
        ),
    )(
        jnp.swapaxes(pair_list, 1, 2), flag_list, pair_counts,
        *w_pieces, *pieces,
    )


def solution(mesh):
    total, row_total = mesh.shape["pb"], mesh.shape["row"]

    def shards(orbitals, interaction, pair_list, flag_list, pair_counts):
        rows, width = orbitals.shape[1:]
        fits = total * interaction.shape[3] * width * 2 <= 8 * 2**20
        aligned = rows % 64 == 0 and (CORES * rows) % 128 == 0 and (rows + 64) % 128 == 0
        if row_total == 2 * CORES and total % 2 == 0 and total >= 4 and fits and aligned:
            return paired_shards(
                total, orbitals, interaction, pair_list, flag_list, pair_counts
            )
        return general_shards(orbitals, interaction, pair_list, flag_list, pair_counts)

    return jax.shard_map(
        shards,
        mesh=mesh,
        in_specs=(
            P("pb", "row", None),
            P(None, "pb", "row", None),
            P("pb", None, None),
            P("pb", None),
            P("pb"),
        ),
        out_specs=P("pb", None, "row", None),
        check_vma=False,
    )
```

```python
import functools

import jax
import jax.numpy as jnp
from jax import lax
from jax.experimental import pallas as pl
from jax.experimental.pallas import tpu as pltpu
from jax.sharding import PartitionSpec as P

CORES = 2


def rotate_parts(block):
    half_width = block.shape[1] // 2
    return jnp.concatenate([block[:, half_width:], -block[:, :half_width]], axis=1)


def apply_kernel(kern_real, kern_imag, target):
    half_width = target.shape[1] // 2
    prod_real = jnp.dot(kern_real, target, preferred_element_type=jnp.float32)
    prod_imag = jnp.dot(kern_imag, target, preferred_element_type=jnp.float32)
    return jnp.concatenate(
        [
            prod_real[:, :half_width] - prod_imag[:, half_width:],
            prod_real[:, half_width:] + prod_imag[:, :half_width],
        ],
        axis=1,
    )


def density(local_rows, all_rows):
    dens_real = jnp.dot(local_rows, all_rows.T, preferred_element_type=jnp.float32)
    dens_imag = jnp.dot(rotate_parts(local_rows), all_rows.T, preferred_element_type=jnp.float32)
    return (dens_real, dens_imag)


def general_shards(orbitals, interaction, pair_list, flag_list, pair_counts):
    slot_total = pair_list.shape[1]
    wanted = jnp.stack([pair_list[0, :, 0], pair_list[0, :, 1]])
    shard_piece = lax.all_gather(orbitals, "pb", axis=0, tiled=True)
    indices = jnp.arange(shard_piece.shape[0], dtype=jnp.int32)
    select = (wanted[:, :, None] == indices[None, None, :]).astype(jnp.bfloat16)
    chosen = jnp.einsum(
        "spi,ird->sprd", select, shard_piece, preferred_element_type=jnp.float32
    ).astype(jnp.bfloat16)
    all_rows = lax.all_gather(chosen, "row", axis=2, tiled=True)
    w_real = interaction[0, 0]
    w_imag = interaction[1, 0]
    active = jnp.arange(slot_total) < pair_counts[0]
    adjoint = flag_list[0] == 1
    turned = lax.all_to_all(interaction[:, 0], "row", split_axis=2, concat_axis=1, tiled=True)
    turned = jnp.swapaxes(turned, 1, 2)
    results = []
    for slot_index in range(slot_total):
        dens_real, dens_imag = density(chosen[1, slot_index], all_rows[1, slot_index])
        eff_real = jnp.where(adjoint[slot_index], turned[0], w_real)
        eff_imag = jnp.where(adjoint[slot_index], -turned[1], w_imag)
        kern_real = (eff_real * dens_real - eff_imag * dens_imag).astype(jnp.bfloat16)
        kern_imag = (eff_real * dens_imag + eff_imag * dens_real).astype(jnp.bfloat16)
        keep_slot = active[slot_index].astype(jnp.float32)
        results.append(apply_kernel(kern_real, kern_imag, all_rows[0, slot_index]) * keep_slot)
    output = jnp.stack(results)
    return output[None]


def ring_position(index, total):
    half = index // 2
    return jnp.where(index % 2 == 0, half, total - 1 - half)


def ring_order(total):
    return list(range(0, total, 2)) + list(range(total - 1, 0, -2))


def rotated(block):
    half = block.shape[1] // 2
    return jnp.concatenate([block[:, half:], -block[:, :half]], axis=1)


def exchange_kernel(steps, total, *refs):
    (pairs, flags, counts), refs = refs[:3], refs[3:]
    (w_own, w_core, w_far, w_far_core), refs = refs[:4], refs[4:]
    near, refs = refs[:2], refs[2:]
    ring, refs = refs[: 2 * steps], refs[2 * steps :]
    swap, refs = refs[: 2 * steps], refs[2 * steps :]
    last, refs = refs[:2], refs[2:]
    out, eff, full, orb_sem = refs
    slots, rows, width = out.shape[1:]
    points = full.shape[2]
    chip = 2 * rows
    wide = rows + 64
    row = lax.axis_index("row")
    x, c = row // CORES, row % CORES
    me = ring_position(lax.axis_index("pb"), total)

    def fetch(slot):
        turned = flags[0, slot] == 1
        for which in (1, 0):
            momentum = pairs[0, which, slot]
            spot = jnp.where(momentum % 2 == 0, momentum // 2, total - 1 - momentum // 2)
            gap = lax.rem(spot - me + total, total)
            dst, sem = full.at[which, slot], orb_sem.at[which, slot]

            def bring(waves, dst=dst, sem=sem):
                for wave in range(2):
                    at = jnp.where(turned, wave, jnp.where(wave == 0, x, 1 - x)) * chip
                    pltpu.make_async_copy(
                        waves[wave], dst.at[pl.ds(pl.multiple_of(at, chip), chip)], sem
                    ).start()

            pl.when(gap == 0)(functools.partial(bring, near))
            for k in range(1, steps + 1):
                own = gap == jnp.where(c == 0, total - k, k)
                other = gap == jnp.where(c == 0, k, total - k)
                pl.when(own)(functools.partial(bring, ring[2 * k - 2 : 2 * k]))
                pl.when(other)(functools.partial(bring, swap[2 * k - 2 : 2 * k]))
            pl.when(gap == steps + 1)(functools.partial(bring, last))

    def arrive(which, slot):
        pltpu.make_async_copy(
            full.at[which, slot], full.at[which, slot], orb_sem.at[which, slot]
        ).wait()

    fetch(0)
    for slot in range(1, slots):
        fetch(slot)
    any_turned = False
    for slot in range(slots):
        any_turned = jnp.logical_or(
            any_turned, jnp.logical_and(slot < counts[0], flags[0, slot] == 1)
        )
    for core in range(CORES):

        @pl.when(jnp.logical_and(any_turned, c == core))
        def _(core=core):
            first = core * (chip - wide)
            start = pl.multiple_of(x * chip + first, 128)
            skip = core * (wide - rows)
            for block, lanes, at in (
                (w_own.at[:, 0], pl.ds(start, wide), core * rows),
                (w_core, slice(0, wide), (1 - core) * rows),
                (w_far, slice(first, first + wide), chip + core * rows),
                (w_far_core, slice(first, first + wide), chip + (1 - core) * rows),
            ):
                eff[0, :, at : at + rows] = block[0, :, lanes].T[skip : skip + rows]
                eff[1, :, at : at + rows] = -block[1, :, lanes].T[skip : skip + rows]

    def apply(slot, w_real, w_imag, mine):
        local = full[1, slot, pl.ds(pl.multiple_of(mine * rows, rows), rows)]
        left = jnp.concatenate([local, rotated(local)], axis=0)
        step = 128
        result = jnp.zeros((rows, width), jnp.float32)
        for at in range(0, points, step):
            dens = lax.dot_general(
                left,
                full[1, slot, at : at + step],
                (((1,), (1,)), ((), ())),
                preferred_element_type=jnp.float32,
            )
            dens_real, dens_imag = dens[:rows], dens[rows:]
            eff_real = w_real[:, at : at + step].astype(jnp.float32)
            eff_imag = w_imag[:, at : at + step].astype(jnp.float32)
            kern_real = (eff_real * dens_real - eff_imag * dens_imag).astype(jnp.bfloat16)
            kern_imag = (eff_real * dens_imag + eff_imag * dens_real).astype(jnp.bfloat16)
            target = full[0, slot, at : at + step]
            result += jnp.dot(kern_real, target, preferred_element_type=jnp.float32)
            result += jnp.dot(kern_imag, -rotated(target), preferred_element_type=jnp.float32)
        out[0, slot] = result

    def compute(slot, carry):
        arrive(1, slot)
        arrive(0, slot)
        live = slot < counts[0]
        turned = flags[0, slot] == 1

        @pl.when(jnp.logical_and(live, jnp.logical_not(turned)))
        def _():
            apply(slot, w_own.at[0, 0], w_own.at[1, 0], 2 * x + c)

        @pl.when(jnp.logical_and(live, turned))
        def _():
            apply(slot, eff.at[0], eff.at[1], c)

        @pl.when(jnp.logical_not(live))
        def _():
            out[0, slot] = jnp.zeros((rows, width), jnp.float32)

        return carry

    lax.fori_loop(0, slots, compute, 0)


def paired_shards(total, orbitals, interaction, pair_list, flag_list, pair_counts):
    _, rows, width = orbitals.shape
    slots = pair_list.shape[1]
    points = interaction.shape[3]
    chip = CORES * rows
    row = lax.axis_index("row")
    x, c = row // CORES, row % CORES
    order = ring_order(total)
    row_total = 2 * CORES

    def other_core(value):
        return lax.ppermute(value, "row", [(r, r ^ 1) for r in range(row_total)])

    def other_chip(value):
        return lax.ppermute(value, "row", [(r, r ^ CORES) for r in range(row_total)])

    def along_ring(value):
        moves = []
        for place in range(total):
            for r in range(row_total):
                step = 1 if r % CORES == 0 else -1
                target = order[(place + step) % total]
                moves.append((order[place] * row_total + r, target * row_total + r))
        return lax.ppermute(value, ("pb", "row"), moves)

    def in_order(mine, other):
        return jnp.where(
            c == 0, jnp.concatenate([mine, other]), jnp.concatenate([other, mine])
        )

    def after(value, *earlier):
        return lax.optimization_barrier((value, *earlier))[0]

    own = orbitals[0]
    w_block = interaction[:, 0]
    far = other_chip(own)
    near_other = other_core(own)
    near = [in_order(own, near_other)]
    w_away = lax.dynamic_slice_in_dim(w_block, (1 - x) * chip, chip, axis=2)
    w_far = other_chip(after(w_away, far))
    near.append(in_order(far, other_core(after(far, w_away))))
    steps = total // 2 - 1
    first, second = [near[0]], [near[1]]
    swap_first, swap_second = [], []
    wide = rows + 64
    w_mine = lax.dynamic_slice_in_dim(w_block, x * chip + (1 - c) * (chip - wide), wide, axis=2)
    for k in range(steps + 1):
        if k == 1:
            w_core = other_core(after(w_mine, first[1]))
        if k >= 2:
            swap_first.append(other_core(first[k - 1]))
            swap_second.append(other_core(second[k - 1]))
        ahead = [*second[k - 1 : k], *(swap_second[:1] if k == 3 else [])] if k else []
        behind = [first[k], *([w_core, *swap_first[:1]] if k == 3 else [])] if k else []
        first.append(along_ring(after(first[k], *ahead)))
        second.append(along_ring(after(second[k], *behind)))
    ring = [wave[k] for k in range(1, steps + 1) for wave in (first, second)]
    last = [first[steps + 1], second[steps + 1]]
    for k in range(len(swap_first) + 1, steps + 1):
        swap_first.append(other_core(after(first[k], last[0])))
        swap_second.append(other_core(after(second[k], *last)))
    swap = [wave[k] for k in range(steps) for wave in (swap_first, swap_second)]
    w_far_core = other_core(after(w_far, *last))

    in_hbm = pl.BlockSpec(memory_space=pltpu.HBM)
    in_vmem = pl.BlockSpec(memory_space=pltpu.VMEM)
    scalars = pl.BlockSpec(memory_space=pltpu.SMEM)
    pieces = [
        pltpu.with_memory_space_constraint(piece, pltpu.HBM)
        for piece in (*near, *ring, *swap, *last)
    ]
    w_pieces = [pltpu.with_memory_space_constraint(piece, pltpu.VMEM) for piece in (interaction, w_core, w_far, w_far_core)]
    return pl.pallas_call(
        functools.partial(exchange_kernel, steps, total),
        out_shape=jax.ShapeDtypeStruct((1, slots, rows, width), jnp.float32),
        in_specs=[scalars] * 3 + [in_vmem] * 4 + [in_hbm] * len(pieces),
        out_specs=in_vmem,
        scratch_shapes=[
            pltpu.VMEM((2, rows, points), jnp.bfloat16),
            pltpu.VMEM((2, slots, points, width), jnp.bfloat16),
            pltpu.SemaphoreType.DMA((2, slots)),
        ],
        compiler_params=pltpu.CompilerParams(vmem_limit_bytes=24 * 2**20),
        cost_estimate=pl.CostEstimate(
            flops=slots * rows * points * width * 8, bytes_accessed=8 * 2**20, transcendentals=0
        ),
    )(
        jnp.swapaxes(pair_list, 1, 2), flag_list, pair_counts,
        *w_pieces, *pieces,
    )


def solution(mesh):
    total, row_total = mesh.shape["pb"], mesh.shape["row"]

    def shards(orbitals, interaction, pair_list, flag_list, pair_counts):
        rows, width = orbitals.shape[1:]
        fits = total * interaction.shape[3] * width * 2 <= 8 * 2**20
        aligned = rows % 64 == 0 and (CORES * rows) % 128 == 0 and (rows + 64) % 128 == 0
        if row_total == 2 * CORES and total % 2 == 0 and total >= 4 and fits and aligned:
            return paired_shards(
                total, orbitals, interaction, pair_list, flag_list, pair_counts
            )
        return general_shards(orbitals, interaction, pair_list, flag_list, pair_counts)

    return jax.shard_map(
        shards,
        mesh=mesh,
        in_specs=(
            P("pb", "row", None),
            P(None, "pb", "row", None),
            P("pb", None, None),
            P("pb", None),
            P("pb"),
        ),
        out_specs=P("pb", None, "row", None),
        check_vma=False,
    )
```

```python
import functools

import jax
import jax.numpy as jnp
from jax import lax
from jax.experimental import pallas as pl
from jax.experimental.pallas import tpu as pltpu
from jax.sharding import PartitionSpec as P

CORES = 2


def rotate_parts(block):
    half_width = block.shape[1] // 2
    return jnp.concatenate([block[:, half_width:], -block[:, :half_width]], axis=1)


def apply_kernel(kern_real, kern_imag, target):
    half_width = target.shape[1] // 2
    prod_real = jnp.dot(kern_real, target, preferred_element_type=jnp.float32)
    prod_imag = jnp.dot(kern_imag, target, preferred_element_type=jnp.float32)
    return jnp.concatenate(
        [
            prod_real[:, :half_width] - prod_imag[:, half_width:],
            prod_real[:, half_width:] + prod_imag[:, :half_width],
        ],
        axis=1,
    )


def density(local_rows, all_rows):
    dens_real = jnp.dot(local_rows, all_rows.T, preferred_element_type=jnp.float32)
    dens_imag = jnp.dot(rotate_parts(local_rows), all_rows.T, preferred_element_type=jnp.float32)
    return (dens_real, dens_imag)


def general_shards(orbitals, interaction, pair_list, flag_list, pair_counts):
    slot_total = pair_list.shape[1]
    wanted = jnp.stack([pair_list[0, :, 0], pair_list[0, :, 1]])
    shard_piece = lax.all_gather(orbitals, "pb", axis=0, tiled=True)
    indices = jnp.arange(shard_piece.shape[0], dtype=jnp.int32)
    select = (wanted[:, :, None] == indices[None, None, :]).astype(jnp.bfloat16)
    chosen = jnp.einsum(
        "spi,ird->sprd", select, shard_piece, preferred_element_type=jnp.float32
    ).astype(jnp.bfloat16)
    all_rows = lax.all_gather(chosen, "row", axis=2, tiled=True)
    w_real = interaction[0, 0]
    w_imag = interaction[1, 0]
    active = jnp.arange(slot_total) < pair_counts[0]
    adjoint = flag_list[0] == 1
    turned = lax.all_to_all(interaction[:, 0], "row", split_axis=2, concat_axis=1, tiled=True)
    turned = jnp.swapaxes(turned, 1, 2)
    results = []
    for slot_index in range(slot_total):
        dens_real, dens_imag = density(chosen[1, slot_index], all_rows[1, slot_index])
        eff_real = jnp.where(adjoint[slot_index], turned[0], w_real)
        eff_imag = jnp.where(adjoint[slot_index], -turned[1], w_imag)
        kern_real = (eff_real * dens_real - eff_imag * dens_imag).astype(jnp.bfloat16)
        kern_imag = (eff_real * dens_imag + eff_imag * dens_real).astype(jnp.bfloat16)
        keep_slot = active[slot_index].astype(jnp.float32)
        results.append(apply_kernel(kern_real, kern_imag, all_rows[0, slot_index]) * keep_slot)
    output = jnp.stack(results)
    return output[None]


def ring_position(index, total):
    half = index // 2
    return jnp.where(index % 2 == 0, half, total - 1 - half)


def ring_order(total):
    return list(range(0, total, 2)) + list(range(total - 1, 0, -2))


def rotated(block):
    half = block.shape[1] // 2
    return jnp.concatenate([block[:, half:], -block[:, :half]], axis=1)


def exchange_kernel(steps, total, *refs):
    (pairs, flags, counts), refs = refs[:3], refs[3:]
    (w_own, w_core, w_far, w_far_core), refs = refs[:4], refs[4:]
    near, refs = refs[:2], refs[2:]
    ring, refs = refs[: 2 * steps], refs[2 * steps :]
    swap, refs = refs[: 2 * steps], refs[2 * steps :]
    last, refs = refs[:2], refs[2:]
    out, eff, full, orb_sem = refs
    slots, rows, width = out.shape[1:]
    points = full.shape[2]
    chip = 2 * rows
    wide = rows + 64
    row = lax.axis_index("row")
    x, c = row // CORES, row % CORES
    me = ring_position(lax.axis_index("pb"), total)

    def fetch(slot):
        turned = flags[0, slot] == 1
        for which in (1, 0):
            momentum = pairs[0, which, slot]
            spot = jnp.where(momentum % 2 == 0, momentum // 2, total - 1 - momentum // 2)
            gap = lax.rem(spot - me + total, total)
            dst, sem = full.at[which, slot], orb_sem.at[which, slot]

            def bring(waves, core=c, dst=dst, sem=sem):
                for wave in range(2):
                    block = jnp.where(turned, wave, jnp.where(wave == 0, x, 1 - x))
                    for part, unit in ((0, core), (1, 1 - core)):
                        at = pl.multiple_of((CORES * block + unit) * rows, rows)
                        pltpu.make_async_copy(
                            waves[wave].at[pl.ds(part * rows, rows)], dst.at[pl.ds(at, rows)], sem
                        ).start()

            pl.when(gap == 0)(functools.partial(bring, near))
            for k in range(1, steps + 1):
                own = gap == jnp.where(c == 0, total - k, k)
                other = gap == jnp.where(c == 0, k, total - k)
                pl.when(own)(functools.partial(bring, ring[2 * k - 2 : 2 * k]))
                pl.when(other)(functools.partial(bring, swap[2 * k - 2 : 2 * k], 1 - c))
            pl.when(gap == steps + 1)(functools.partial(bring, last))

    def arrive(which, slot):
        pltpu.make_async_copy(
            full.at[which, slot], full.at[which, slot], orb_sem.at[which, slot]
        ).wait()

    fetch(0)
    for slot in range(1, slots):
        fetch(slot)
    any_turned = False
    for slot in range(slots):
        any_turned = jnp.logical_or(
            any_turned, jnp.logical_and(slot < counts[0], flags[0, slot] == 1)
        )
    for core in range(CORES):

        @pl.when(jnp.logical_and(any_turned, c == core))
        def _(core=core):
            first = core * (chip - wide)
            start = pl.multiple_of(x * chip + first, 128)
            skip = core * (wide - rows)
            for block, lanes, at in (
                (w_own.at[:, 0], pl.ds(start, wide), core * rows),
                (w_core, slice(0, wide), (1 - core) * rows),
                (w_far, slice(first, first + wide), chip + core * rows),
                (w_far_core, slice(first, first + wide), chip + (1 - core) * rows),
            ):
                eff[0, :, at : at + rows] = block[0, :, lanes].T[skip : skip + rows]
                eff[1, :, at : at + rows] = -block[1, :, lanes].T[skip : skip + rows]

    def apply(slot, w_real, w_imag, mine):
        local = full[1, slot, pl.ds(pl.multiple_of(mine * rows, rows), rows)]
        left = jnp.concatenate([local, rotated(local)], axis=0)
        step = 128
        result = jnp.zeros((rows, width), jnp.float32)
        for at in range(0, points, step):
            dens = lax.dot_general(
                left,
                full[1, slot, at : at + step],
                (((1,), (1,)), ((), ())),
                preferred_element_type=jnp.float32,
            )
            dens_real, dens_imag = dens[:rows], dens[rows:]
            eff_real = w_real[:, at : at + step].astype(jnp.float32)
            eff_imag = w_imag[:, at : at + step].astype(jnp.float32)
            kern_real = (eff_real * dens_real - eff_imag * dens_imag).astype(jnp.bfloat16)
            kern_imag = (eff_real * dens_imag + eff_imag * dens_real).astype(jnp.bfloat16)
            target = full[0, slot, at : at + step]
            result += jnp.dot(kern_real, target, preferred_element_type=jnp.float32)
            result += jnp.dot(kern_imag, -rotated(target), preferred_element_type=jnp.float32)
        out[0, slot] = result

    def compute(slot, carry):
        arrive(1, slot)
        arrive(0, slot)
        live = slot < counts[0]
        turned = flags[0, slot] == 1

        @pl.when(jnp.logical_and(live, jnp.logical_not(turned)))
        def _():
            apply(slot, w_own.at[0, 0], w_own.at[1, 0], 2 * x + c)

        @pl.when(jnp.logical_and(live, turned))
        def _():
            apply(slot, eff.at[0], eff.at[1], c)

        @pl.when(jnp.logical_not(live))
        def _():
            out[0, slot] = jnp.zeros((rows, width), jnp.float32)

        return carry

    lax.fori_loop(0, slots, compute, 0)


def paired_shards(total, orbitals, interaction, pair_list, flag_list, pair_counts):
    _, rows, width = orbitals.shape
    slots = pair_list.shape[1]
    points = interaction.shape[3]
    chip = CORES * rows
    row = lax.axis_index("row")
    x, c = row // CORES, row % CORES
    order = ring_order(total)
    row_total = 2 * CORES

    def other_core(value):
        return lax.ppermute(value, "row", [(r, r ^ 1) for r in range(row_total)])

    def other_chip(value):
        return lax.ppermute(value, "row", [(r, r ^ CORES) for r in range(row_total)])

    def along_ring(value):
        moves = []
        for place in range(total):
            for r in range(row_total):
                step = 1 if r % CORES == 0 else -1
                target = order[(place + step) % total]
                moves.append((order[place] * row_total + r, target * row_total + r))
        return lax.ppermute(value, ("pb", "row"), moves)

    def after(value, *earlier):
        return lax.optimization_barrier((value, *earlier))[0]

    own = orbitals[0]
    w_block = interaction[:, 0]
    far = other_chip(own)
    near_other = other_core(own)
    near = [jnp.concatenate([own, near_other])]
    w_away = lax.dynamic_slice_in_dim(w_block, (1 - x) * chip, chip, axis=2)
    w_far = other_chip(after(w_away, far))
    near.append(jnp.concatenate([far, other_core(after(far, w_away))]))
    steps = total // 2 - 1
    first, second = [near[0]], [near[1]]
    swap_first, swap_second = [], []
    wide = rows + 64
    w_mine = lax.dynamic_slice_in_dim(w_block, x * chip + (1 - c) * (chip - wide), wide, axis=2)
    for k in range(steps + 1):
        if k == 1:
            w_core = other_core(after(w_mine, first[1]))
        if k == 2:
            swap_first.append(other_core(first[k - 1]))
            swap_second.append(other_core(second[k - 1]))
        ahead = [*second[k - 1 : k], *(swap_second[:1] if k == 3 else [])] if k else []
        behind = [first[k], *([w_core, *swap_first[:1]] if k == 3 else [])] if k else []
        first.append(along_ring(after(first[k], *ahead)))
        second.append(along_ring(after(second[k], *behind)))
    ring = [wave[k] for k in range(1, steps + 1) for wave in (first, second)]
    last = [first[steps + 1], second[steps + 1]]
    swap_first.append(other_core(after(first[steps - 1], last[0])))
    swap_second.append(other_core(after(second[steps - 1], *last)))
    swap_first.append(other_core(after(first[steps], last[0])))
    swap_second.append(other_core(after(second[steps], *last)))
    swap = [wave[k] for k in range(steps) for wave in (swap_first, swap_second)]
    w_far_core = other_core(after(w_far, *last))

    in_hbm = pl.BlockSpec(memory_space=pltpu.HBM)
    in_vmem = pl.BlockSpec(memory_space=pltpu.VMEM)
    scalars = pl.BlockSpec(memory_space=pltpu.SMEM)
    pieces = [
        pltpu.with_memory_space_constraint(piece, pltpu.HBM)
        for piece in (*near, *ring, *swap, *last)
    ]
    w_pieces = [pltpu.with_memory_space_constraint(piece, pltpu.VMEM) for piece in (interaction, w_core, w_far, w_far_core)]
    return pl.pallas_call(
        functools.partial(exchange_kernel, steps, total),
        out_shape=jax.ShapeDtypeStruct((1, slots, rows, width), jnp.float32),
        in_specs=[scalars] * 3 + [in_vmem] * 4 + [in_hbm] * len(pieces),
        out_specs=in_vmem,
        scratch_shapes=[
            pltpu.VMEM((2, rows, points), jnp.bfloat16),
            pltpu.VMEM((2, slots, points, width), jnp.bfloat16),
            pltpu.SemaphoreType.DMA((2, slots)),
        ],
        compiler_params=pltpu.CompilerParams(vmem_limit_bytes=24 * 2**20),
        cost_estimate=pl.CostEstimate(
            flops=slots * rows * points * width * 8, bytes_accessed=8 * 2**20, transcendentals=0
        ),
    )(
        jnp.swapaxes(pair_list, 1, 2), flag_list, pair_counts,
        *w_pieces, *pieces,
    )


def solution(mesh):
    total, row_total = mesh.shape["pb"], mesh.shape["row"]

    def shards(orbitals, interaction, pair_list, flag_list, pair_counts):
        rows, width = orbitals.shape[1:]
        fits = total * interaction.shape[3] * width * 2 <= 8 * 2**20
        aligned = rows % 64 == 0 and (CORES * rows) % 128 == 0 and (rows + 64) % 128 == 0
        if row_total == 2 * CORES and total % 2 == 0 and total >= 4 and fits and aligned:
            return paired_shards(
                total, orbitals, interaction, pair_list, flag_list, pair_counts
            )
        return general_shards(orbitals, interaction, pair_list, flag_list, pair_counts)

    return jax.shard_map(
        shards,
        mesh=mesh,
        in_specs=(
            P("pb", "row", None),
            P(None, "pb", "row", None),
            P("pb", None, None),
            P("pb", None),
            P("pb"),
        ),
        out_specs=P("pb", None, "row", None),
        check_vma=False,
    )
```

```python
import functools

import jax
import jax.numpy as jnp
from jax import lax
from jax.experimental import pallas as pl
from jax.experimental.pallas import tpu as pltpu
from jax.sharding import PartitionSpec as P

CORES = 2


def rotate_parts(block):
    half_width = block.shape[1] // 2
    return jnp.concatenate([block[:, half_width:], -block[:, :half_width]], axis=1)


def apply_kernel(kern_real, kern_imag, target):
    half_width = target.shape[1] // 2
    prod_real = jnp.dot(kern_real, target, preferred_element_type=jnp.float32)
    prod_imag = jnp.dot(kern_imag, target, preferred_element_type=jnp.float32)
    return jnp.concatenate(
        [
            prod_real[:, :half_width] - prod_imag[:, half_width:],
            prod_real[:, half_width:] + prod_imag[:, :half_width],
        ],
        axis=1,
    )


def density(local_rows, all_rows):
    dens_real = jnp.dot(local_rows, all_rows.T, preferred_element_type=jnp.float32)
    dens_imag = jnp.dot(rotate_parts(local_rows), all_rows.T, preferred_element_type=jnp.float32)
    return (dens_real, dens_imag)


def general_shards(orbitals, interaction, pair_list, flag_list, pair_counts):
    slot_total = pair_list.shape[1]
    wanted = jnp.stack([pair_list[0, :, 0], pair_list[0, :, 1]])
    shard_piece = lax.all_gather(orbitals, "pb", axis=0, tiled=True)
    indices = jnp.arange(shard_piece.shape[0], dtype=jnp.int32)
    select = (wanted[:, :, None] == indices[None, None, :]).astype(jnp.bfloat16)
    chosen = jnp.einsum(
        "spi,ird->sprd", select, shard_piece, preferred_element_type=jnp.float32
    ).astype(jnp.bfloat16)
    all_rows = lax.all_gather(chosen, "row", axis=2, tiled=True)
    w_real = interaction[0, 0]
    w_imag = interaction[1, 0]
    active = jnp.arange(slot_total) < pair_counts[0]
    adjoint = flag_list[0] == 1
    turned = lax.all_to_all(interaction[:, 0], "row", split_axis=2, concat_axis=1, tiled=True)
    turned = jnp.swapaxes(turned, 1, 2)
    results = []
    for slot_index in range(slot_total):
        dens_real, dens_imag = density(chosen[1, slot_index], all_rows[1, slot_index])
        eff_real = jnp.where(adjoint[slot_index], turned[0], w_real)
        eff_imag = jnp.where(adjoint[slot_index], -turned[1], w_imag)
        kern_real = (eff_real * dens_real - eff_imag * dens_imag).astype(jnp.bfloat16)
        kern_imag = (eff_real * dens_imag + eff_imag * dens_real).astype(jnp.bfloat16)
        keep_slot = active[slot_index].astype(jnp.float32)
        results.append(apply_kernel(kern_real, kern_imag, all_rows[0, slot_index]) * keep_slot)
    output = jnp.stack(results)
    return output[None]


def ring_position(index, total):
    half = index // 2
    return jnp.where(index % 2 == 0, half, total - 1 - half)


def ring_order(total):
    return list(range(0, total, 2)) + list(range(total - 1, 0, -2))


def rotated(block):
    half = block.shape[1] // 2
    return jnp.concatenate([block[:, half:], -block[:, :half]], axis=1)


def exchange_kernel(steps, total, *refs):
    (pairs, flags, counts), refs = refs[:3], refs[3:]
    (w_own, w_core, w_far, w_far_core), refs = refs[:4], refs[4:]
    near, refs = refs[:2], refs[2:]
    ring, refs = refs[: 2 * steps], refs[2 * steps :]
    swap, refs = refs[: 2 * steps], refs[2 * steps :]
    last, refs = refs[:2], refs[2:]
    out_hbm, out, eff, full, orb_sem, out_sem = refs
    slots, rows, width = out.shape
    points = full.shape[2]
    chip = 2 * rows
    wide = rows + 64
    row = lax.axis_index("row")
    x, c = row // CORES, row % CORES
    me = ring_position(lax.axis_index("pb"), total)

    def fetch(slot):
        turned = flags[0, slot] == 1
        for which in (1, 0):
            momentum = pairs[0, which, slot]
            spot = jnp.where(momentum % 2 == 0, momentum // 2, total - 1 - momentum // 2)
            gap = lax.rem(spot - me + total, total)
            dst, sem = full.at[which, slot], orb_sem.at[which, slot]

            def bring(waves, core=c, dst=dst, sem=sem):
                for wave in range(2):
                    block = jnp.where(turned, wave, jnp.where(wave == 0, x, 1 - x))
                    for part, unit in ((0, core), (1, 1 - core)):
                        at = pl.multiple_of((CORES * block + unit) * rows, rows)
                        pltpu.make_async_copy(
                            waves[wave].at[pl.ds(part * rows, rows)], dst.at[pl.ds(at, rows)], sem
                        ).start()

            pl.when(gap == 0)(functools.partial(bring, near))
            for k in range(1, steps + 1):
                own = gap == jnp.where(c == 0, total - k, k)
                other = gap == jnp.where(c == 0, k, total - k)
                pl.when(own)(functools.partial(bring, ring[2 * k - 2 : 2 * k]))
                pl.when(other)(functools.partial(bring, swap[2 * k - 2 : 2 * k], 1 - c))
            pl.when(gap == steps + 1)(functools.partial(bring, last))

    def arrive(which, slot):
        pltpu.make_async_copy(
            full.at[which, slot], full.at[which, slot], orb_sem.at[which, slot]
        ).wait()

    fetch(0)
    for slot in range(1, slots):
        fetch(slot)
    any_turned = False
    for slot in range(slots):
        any_turned = jnp.logical_or(
            any_turned, jnp.logical_and(slot < counts[0], flags[0, slot] == 1)
        )
    for core in range(CORES):

        @pl.when(jnp.logical_and(any_turned, c == core))
        def _(core=core):
            first = core * (chip - wide)
            start = pl.multiple_of(x * chip + first, 128)
            skip = core * (wide - rows)
            for block, lanes, at in (
                (w_own.at[:, 0], pl.ds(start, wide), core * rows),
                (w_core, slice(0, wide), (1 - core) * rows),
                (w_far, slice(first, first + wide), chip + core * rows),
                (w_far_core, slice(first, first + wide), chip + (1 - core) * rows),
            ):
                eff[0, :, at : at + rows] = block[0, :, lanes].T[skip : skip + rows]
                eff[1, :, at : at + rows] = -block[1, :, lanes].T[skip : skip + rows]

    def apply(slot, w_real, w_imag, mine):
        local = full[1, slot, pl.ds(pl.multiple_of(mine * rows, rows), rows)]
        left = jnp.concatenate([local, rotated(local)], axis=0)
        step = 128
        result = jnp.zeros((rows, width), jnp.float32)
        for at in range(0, points, step):
            dens = lax.dot_general(
                left,
                full[1, slot, at : at + step],
                (((1,), (1,)), ((), ())),
                preferred_element_type=jnp.float32,
            )
            dens_real, dens_imag = dens[:rows], dens[rows:]
            eff_real = w_real[:, at : at + step].astype(jnp.float32)
            eff_imag = w_imag[:, at : at + step].astype(jnp.float32)
            kern_real = (eff_real * dens_real - eff_imag * dens_imag).astype(jnp.bfloat16)
            kern_imag = (eff_real * dens_imag + eff_imag * dens_real).astype(jnp.bfloat16)
            target = full[0, slot, at : at + step]
            result += jnp.dot(kern_real, target, preferred_element_type=jnp.float32)
            result += jnp.dot(kern_imag, -rotated(target), preferred_element_type=jnp.float32)
        out[slot] = result

    def compute(slot, carry):
        arrive(1, slot)
        arrive(0, slot)
        live = slot < counts[0]
        turned = flags[0, slot] == 1

        @pl.when(jnp.logical_and(live, jnp.logical_not(turned)))
        def _():
            apply(slot, w_own.at[0, 0], w_own.at[1, 0], 2 * x + c)

        @pl.when(jnp.logical_and(live, turned))
        def _():
            apply(slot, eff.at[0], eff.at[1], c)

        @pl.when(jnp.logical_not(live))
        def _():
            out[slot] = jnp.zeros((rows, width), jnp.float32)

        pltpu.make_async_copy(out.at[slot], out_hbm.at[0, slot], out_sem.at[slot]).start()
        return carry

    lax.fori_loop(0, slots, compute, 0)
    for slot in range(slots):
        pltpu.make_async_copy(out.at[slot], out_hbm.at[0, slot], out_sem.at[slot]).wait()


def paired_shards(total, orbitals, interaction, pair_list, flag_list, pair_counts):
    _, rows, width = orbitals.shape
    slots = pair_list.shape[1]
    points = interaction.shape[3]
    chip = CORES * rows
    row = lax.axis_index("row")
    x, c = row // CORES, row % CORES
    order = ring_order(total)
    row_total = 2 * CORES

    def other_core(value):
        return lax.ppermute(value, "row", [(r, r ^ 1) for r in range(row_total)])

    def other_chip(value):
        return lax.ppermute(value, "row", [(r, r ^ CORES) for r in range(row_total)])

    def along_ring(value):
        moves = []
        for place in range(total):
            for r in range(row_total):
                step = 1 if r % CORES == 0 else -1
                target = order[(place + step) % total]
                moves.append((order[place] * row_total + r, target * row_total + r))
        return lax.ppermute(value, ("pb", "row"), moves)

    def after(value, *earlier):
        return lax.optimization_barrier((value, *earlier))[0]

    own = orbitals[0]
    w_block = interaction[:, 0]
    far = other_chip(own)
    near_other = other_core(own)
    near = [jnp.concatenate([own, near_other])]
    w_away = lax.dynamic_slice_in_dim(w_block, (1 - x) * chip, chip, axis=2)
    w_far = other_chip(after(w_away, far))
    near.append(jnp.concatenate([far, other_core(after(far, w_away))]))
    steps = total // 2 - 1
    first, second = [near[0]], [near[1]]
    swap_first, swap_second = [], []
    wide = rows + 64
    w_mine = lax.dynamic_slice_in_dim(w_block, x * chip + (1 - c) * (chip - wide), wide, axis=2)
    for k in range(steps + 1):
        if k == 1:
            w_core = other_core(after(w_mine, first[1]))
        if k == 2:
            swap_first.append(other_core(first[k - 1]))
            swap_second.append(other_core(second[k - 1]))
        ahead = [*second[k - 1 : k], *(swap_second[:1] if k == 3 else [])] if k else []
        behind = [first[k], *([w_core, *swap_first[:1]] if k == 3 else [])] if k else []
        first.append(along_ring(after(first[k], *ahead)))
        second.append(along_ring(after(second[k], *behind)))
    ring = [wave[k] for k in range(1, steps + 1) for wave in (first, second)]
    last = [first[steps + 1], second[steps + 1]]
    swap_first.append(other_core(after(first[steps - 1], last[0])))
    swap_second.append(other_core(after(second[steps - 1], *last)))
    swap_first.append(other_core(after(first[steps], last[0])))
    swap_second.append(other_core(after(second[steps], *last)))
    swap = [wave[k] for k in range(steps) for wave in (swap_first, swap_second)]
    w_far_core = other_core(after(w_far, *last))

    in_hbm = pl.BlockSpec(memory_space=pltpu.HBM)
    in_vmem = pl.BlockSpec(memory_space=pltpu.VMEM)
    scalars = pl.BlockSpec(memory_space=pltpu.SMEM)
    pieces = [
        pltpu.with_memory_space_constraint(piece, pltpu.HBM)
        for piece in (*near, *ring, *swap, *last)
    ]
    w_pieces = [pltpu.with_memory_space_constraint(piece, pltpu.VMEM) for piece in (interaction, w_core, w_far, w_far_core)]
    return pl.pallas_call(
        functools.partial(exchange_kernel, steps, total),
        out_shape=jax.ShapeDtypeStruct((1, slots, rows, width), jnp.float32),
        in_specs=[scalars] * 3 + [in_vmem] * 4 + [in_hbm] * len(pieces),
        out_specs=in_hbm,
        scratch_shapes=[
            pltpu.VMEM((slots, rows, width), jnp.float32),
            pltpu.VMEM((2, rows, points), jnp.bfloat16),
            pltpu.VMEM((2, slots, points, width), jnp.bfloat16),
            pltpu.SemaphoreType.DMA((2, slots)),
            pltpu.SemaphoreType.DMA((slots,)),
        ],
        compiler_params=pltpu.CompilerParams(vmem_limit_bytes=24 * 2**20),
        cost_estimate=pl.CostEstimate(
            flops=slots * rows * points * width * 8, bytes_accessed=8 * 2**20, transcendentals=0
        ),
    )(
        jnp.swapaxes(pair_list, 1, 2), flag_list, pair_counts,
        *w_pieces, *pieces,
    )


def solution(mesh):
    total, row_total = mesh.shape["pb"], mesh.shape["row"]

    def shards(orbitals, interaction, pair_list, flag_list, pair_counts):
        rows, width = orbitals.shape[1:]
        fits = total * interaction.shape[3] * width * 2 <= 8 * 2**20
        aligned = rows % 64 == 0 and (CORES * rows) % 128 == 0 and (rows + 64) % 128 == 0
        if row_total == 2 * CORES and total % 2 == 0 and total >= 4 and fits and aligned:
            return paired_shards(
                total, orbitals, interaction, pair_list, flag_list, pair_counts
            )
        return general_shards(orbitals, interaction, pair_list, flag_list, pair_counts)

    return jax.shard_map(
        shards,
        mesh=mesh,
        in_specs=(
            P("pb", "row", None),
            P(None, "pb", "row", None),
            P("pb", None, None),
            P("pb", None),
            P("pb"),
        ),
        out_specs=P("pb", None, "row", None),
        check_vma=False,
    )
```

```python
import functools

import jax
import jax.numpy as jnp
from jax import lax
from jax.experimental import pallas as pl
from jax.experimental.pallas import tpu as pltpu
from jax.sharding import PartitionSpec as P

CORES = 2


def rotate_parts(block):
    half_width = block.shape[1] // 2
    return jnp.concatenate([block[:, half_width:], -block[:, :half_width]], axis=1)


def apply_kernel(kern_real, kern_imag, target):
    half_width = target.shape[1] // 2
    prod_real = jnp.dot(kern_real, target, preferred_element_type=jnp.float32)
    prod_imag = jnp.dot(kern_imag, target, preferred_element_type=jnp.float32)
    return jnp.concatenate(
        [
            prod_real[:, :half_width] - prod_imag[:, half_width:],
            prod_real[:, half_width:] + prod_imag[:, :half_width],
        ],
        axis=1,
    )


def density(local_rows, all_rows):
    dens_real = jnp.dot(local_rows, all_rows.T, preferred_element_type=jnp.float32)
    dens_imag = jnp.dot(rotate_parts(local_rows), all_rows.T, preferred_element_type=jnp.float32)
    return (dens_real, dens_imag)


def general_shards(orbitals, interaction, pair_list, flag_list, pair_counts):
    slot_total = pair_list.shape[1]
    wanted = jnp.stack([pair_list[0, :, 0], pair_list[0, :, 1]])
    shard_piece = lax.all_gather(orbitals, "pb", axis=0, tiled=True)
    indices = jnp.arange(shard_piece.shape[0], dtype=jnp.int32)
    select = (wanted[:, :, None] == indices[None, None, :]).astype(jnp.bfloat16)
    chosen = jnp.einsum(
        "spi,ird->sprd", select, shard_piece, preferred_element_type=jnp.float32
    ).astype(jnp.bfloat16)
    all_rows = lax.all_gather(chosen, "row", axis=2, tiled=True)
    w_real = interaction[0, 0]
    w_imag = interaction[1, 0]
    active = jnp.arange(slot_total) < pair_counts[0]
    adjoint = flag_list[0] == 1
    turned = lax.all_to_all(interaction[:, 0], "row", split_axis=2, concat_axis=1, tiled=True)
    turned = jnp.swapaxes(turned, 1, 2)
    results = []
    for slot_index in range(slot_total):
        dens_real, dens_imag = density(chosen[1, slot_index], all_rows[1, slot_index])
        eff_real = jnp.where(adjoint[slot_index], turned[0], w_real)
        eff_imag = jnp.where(adjoint[slot_index], -turned[1], w_imag)
        kern_real = (eff_real * dens_real - eff_imag * dens_imag).astype(jnp.bfloat16)
        kern_imag = (eff_real * dens_imag + eff_imag * dens_real).astype(jnp.bfloat16)
        keep_slot = active[slot_index].astype(jnp.float32)
        results.append(apply_kernel(kern_real, kern_imag, all_rows[0, slot_index]) * keep_slot)
    output = jnp.stack(results)
    return output[None]


def ring_position(index, total):
    half = index // 2
    return jnp.where(index % 2 == 0, half, total - 1 - half)


def ring_order(total):
    return list(range(0, total, 2)) + list(range(total - 1, 0, -2))


def rotated(block):
    half = block.shape[1] // 2
    return jnp.concatenate([block[:, half:], -block[:, :half]], axis=1)


def exchange_kernel(steps, total, *refs):
    (pairs, flags, counts), refs = refs[:3], refs[3:]
    (w_own, w_core, w_far, w_far_core), refs = refs[:4], refs[4:]
    near, refs = refs[:2], refs[2:]
    ring, refs = refs[: 2 * steps], refs[2 * steps :]
    swap, refs = refs[: 2 * steps], refs[2 * steps :]
    last, refs = refs[:2], refs[2:]
    out_hbm, out, eff, full, orb_sem, out_sem = refs
    slots, rows, width = out.shape
    points = full.shape[2]
    chip = 2 * rows
    wide = rows + 64
    row = lax.axis_index("row")
    x, c = row // CORES, row % CORES
    me = ring_position(lax.axis_index("pb"), total)

    def fetch(slot):
        turned = flags[0, slot] == 1
        for which in (1, 0):
            momentum = pairs[0, which, slot]
            spot = jnp.where(momentum % 2 == 0, momentum // 2, total - 1 - momentum // 2)
            gap = lax.rem(spot - me + total, total)
            dst, sem = full.at[which, slot], orb_sem.at[which, slot]

            def bring(waves, core=c, dst=dst, sem=sem):
                for wave in range(2):
                    block = jnp.where(turned, wave, jnp.where(wave == 0, x, 1 - x))
                    for part, unit in ((0, core), (1, 1 - core)):
                        at = pl.multiple_of((CORES * block + unit) * rows, rows)
                        pltpu.make_async_copy(
                            waves[wave].at[pl.ds(part * rows, rows)], dst.at[pl.ds(at, rows)], sem
                        ).start()

            pl.when(gap == 0)(functools.partial(bring, near))
            for k in range(1, steps + 1):
                own = gap == jnp.where(c == 0, total - k, k)
                other = gap == jnp.where(c == 0, k, total - k)
                pl.when(own)(functools.partial(bring, ring[2 * k - 2 : 2 * k]))
                pl.when(other)(functools.partial(bring, swap[2 * k - 2 : 2 * k], 1 - c))
            pl.when(gap == steps + 1)(functools.partial(bring, last))

    def arrive(which, slot):
        pltpu.make_async_copy(
            full.at[which, slot], full.at[which, slot], orb_sem.at[which, slot]
        ).wait()

    fetch(0)
    any_turned = False
    for slot in range(slots):
        any_turned = jnp.logical_or(
            any_turned, jnp.logical_and(slot < counts[0], flags[0, slot] == 1)
        )
    for core in range(CORES):

        @pl.when(jnp.logical_and(any_turned, c == core))
        def _(core=core):
            first = core * (chip - wide)
            start = pl.multiple_of(x * chip + first, 128)
            skip = core * (wide - rows)
            for block, lanes, at in (
                (w_own.at[:, 0], pl.ds(start, wide), core * rows),
                (w_core, slice(0, wide), (1 - core) * rows),
                (w_far, slice(first, first + wide), chip + core * rows),
                (w_far_core, slice(first, first + wide), chip + (1 - core) * rows),
            ):
                eff[0, :, at : at + rows] = block[0, :, lanes].T[skip : skip + rows]
                eff[1, :, at : at + rows] = -block[1, :, lanes].T[skip : skip + rows]

    for slot in range(1, slots):
        fetch(slot)

    def apply(slot, w_real, w_imag, mine):
        local = full[1, slot, pl.ds(pl.multiple_of(mine * rows, rows), rows)]
        left = jnp.concatenate([local, rotated(local)], axis=0)
        step = 128
        result = jnp.zeros((rows, width), jnp.float32)
        for at in range(0, points, step):
            dens = lax.dot_general(
                left,
                full[1, slot, at : at + step],
                (((1,), (1,)), ((), ())),
                preferred_element_type=jnp.float32,
            )
            dens_real, dens_imag = dens[:rows], dens[rows:]
            eff_real = w_real[:, at : at + step].astype(jnp.float32)
            eff_imag = w_imag[:, at : at + step].astype(jnp.float32)
            kern_real = (eff_real * dens_real - eff_imag * dens_imag).astype(jnp.bfloat16)
            kern_imag = (eff_real * dens_imag + eff_imag * dens_real).astype(jnp.bfloat16)
            target = full[0, slot, at : at + step]
            result += jnp.dot(kern_real, target, preferred_element_type=jnp.float32)
            result += jnp.dot(kern_imag, -rotated(target), preferred_element_type=jnp.float32)
        out[slot] = result

    def compute(slot, carry):
        arrive(1, slot)
        arrive(0, slot)
        live = slot < counts[0]
        turned = flags[0, slot] == 1

        @pl.when(jnp.logical_and(live, jnp.logical_not(turned)))
        def _():
            apply(slot, w_own.at[0, 0], w_own.at[1, 0], 2 * x + c)

        @pl.when(jnp.logical_and(live, turned))
        def _():
            apply(slot, eff.at[0], eff.at[1], c)

        @pl.when(jnp.logical_not(live))
        def _():
            out[slot] = jnp.zeros((rows, width), jnp.float32)

        pltpu.make_async_copy(out.at[slot], out_hbm.at[0, slot], out_sem.at[slot]).start()
        return carry

    lax.fori_loop(0, slots, compute, 0)
    for slot in range(slots):
        pltpu.make_async_copy(out.at[slot], out_hbm.at[0, slot], out_sem.at[slot]).wait()


def paired_shards(total, orbitals, interaction, pair_list, flag_list, pair_counts):
    _, rows, width = orbitals.shape
    slots = pair_list.shape[1]
    points = interaction.shape[3]
    chip = CORES * rows
    row = lax.axis_index("row")
    x, c = row // CORES, row % CORES
    order = ring_order(total)
    row_total = 2 * CORES

    def other_core(value):
        return lax.ppermute(value, "row", [(r, r ^ 1) for r in range(row_total)])

    def other_chip(value):
        return lax.ppermute(value, "row", [(r, r ^ CORES) for r in range(row_total)])

    def along_ring(value):
        moves = []
        for place in range(total):
            for r in range(row_total):
                step = 1 if r % CORES == 0 else -1
                target = order[(place + step) % total]
                moves.append((order[place] * row_total + r, target * row_total + r))
        return lax.ppermute(value, ("pb", "row"), moves)

    def after(value, *earlier):
        return lax.optimization_barrier((value, *earlier))[0]

    own = orbitals[0]
    w_block = interaction[:, 0]
    far = other_chip(own)
    near_other = other_core(own)
    near = [jnp.concatenate([own, near_other])]
    w_away = lax.dynamic_slice_in_dim(w_block, (1 - x) * chip, chip, axis=2)
    w_far = other_chip(after(w_away, far))
    near.append(jnp.concatenate([far, other_core(after(far, w_away))]))
    steps = total // 2 - 1
    first, second = [near[0]], [near[1]]
    swap_first, swap_second = [], []
    wide = rows + 64
    w_mine = lax.dynamic_slice_in_dim(w_block, x * chip + (1 - c) * (chip - wide), wide, axis=2)
    for k in range(steps + 1):
        if k == 1:
            w_core = other_core(after(w_mine, first[1]))
        if k == 2:
            swap_first.append(other_core(first[k - 1]))
            swap_second.append(other_core(second[k - 1]))
        ahead = [*second[k - 1 : k], *(swap_second[:1] if k == 3 else [])] if k else []
        behind = [first[k], *([w_core, *swap_first[:1]] if k == 3 else [])] if k else []
        first.append(along_ring(after(first[k], *ahead)))
        second.append(along_ring(after(second[k], *behind)))
    ring = [wave[k] for k in range(1, steps + 1) for wave in (first, second)]
    last = [first[steps + 1], second[steps + 1]]
    swap_first.append(other_core(after(first[steps - 1], last[0])))
    swap_second.append(other_core(after(second[steps - 1], last[0])))
    swap_first.append(other_core(after(first[steps], last[0])))
    swap_second.append(other_core(after(second[steps], *last)))
    swap = [wave[k] for k in range(steps) for wave in (swap_first, swap_second)]
    w_far_core = other_core(after(w_far, *last))

    in_hbm = pl.BlockSpec(memory_space=pltpu.HBM)
    in_vmem = pl.BlockSpec(memory_space=pltpu.VMEM)
    scalars = pl.BlockSpec(memory_space=pltpu.SMEM)
    pieces = [
        pltpu.with_memory_space_constraint(piece, pltpu.HBM)
        for piece in (*near, *ring, *swap, *last)
    ]
    w_pieces = [pltpu.with_memory_space_constraint(piece, pltpu.VMEM) for piece in (interaction, w_core, w_far, w_far_core)]
    return pl.pallas_call(
        functools.partial(exchange_kernel, steps, total),
        out_shape=jax.ShapeDtypeStruct((1, slots, rows, width), jnp.float32),
        in_specs=[scalars] * 3 + [in_vmem] * 4 + [in_hbm] * len(pieces),
        out_specs=in_hbm,
        scratch_shapes=[
            pltpu.VMEM((slots, rows, width), jnp.float32),
            pltpu.VMEM((2, rows, points), jnp.bfloat16),
            pltpu.VMEM((2, slots, points, width), jnp.bfloat16),
            pltpu.SemaphoreType.DMA((2, slots)),
            pltpu.SemaphoreType.DMA((slots,)),
        ],
        compiler_params=pltpu.CompilerParams(vmem_limit_bytes=24 * 2**20),
        cost_estimate=pl.CostEstimate(
            flops=slots * rows * points * width * 8, bytes_accessed=8 * 2**20, transcendentals=0
        ),
    )(
        jnp.swapaxes(pair_list, 1, 2), flag_list, pair_counts,
        *w_pieces, *pieces,
    )


def solution(mesh):
    total, row_total = mesh.shape["pb"], mesh.shape["row"]

    def shards(orbitals, interaction, pair_list, flag_list, pair_counts):
        rows, width = orbitals.shape[1:]
        fits = total * interaction.shape[3] * width * 2 <= 8 * 2**20
        aligned = rows % 64 == 0 and (CORES * rows) % 128 == 0 and (rows + 64) % 128 == 0
        if row_total == 2 * CORES and total % 2 == 0 and total >= 4 and fits and aligned:
            return paired_shards(
                total, orbitals, interaction, pair_list, flag_list, pair_counts
            )
        return general_shards(orbitals, interaction, pair_list, flag_list, pair_counts)

    return jax.shard_map(
        shards,
        mesh=mesh,
        in_specs=(
            P("pb", "row", None),
            P(None, "pb", "row", None),
            P("pb", None, None),
            P("pb", None),
            P("pb"),
        ),
        out_specs=P("pb", None, "row", None),
        check_vma=False,
    )
```
